32 devices in a mesh: grp: 2 (over x), row: 16 (over z, y, core).
Axes of the slice: x: 2, y: 2, z: 4, core: 2. Of those that a mesh axis runs over, the one named last changes fastest.
Arguments:
- frames: bfloat16 [4096, 8192], P('grp', 'row'), parts along dimension 0, may hold values from 0 to 1, as said below
- pattern: int32 [64, 3], P(('grp', 'row')), parts along dimension 0, may hold values from 0 to 1, as said below
- couplings: float32 [64, 3, 256, 256], P(('grp', 'row')), parts along dimension 0, may hold values from -0.7 to 0.7, as said below
- first_moment: float32 [64, 3, 256, 256], P(('grp', 'row')), parts along dimension 0, may hold values from -204.8 to 204.8, as said below
- second_moment: float32 [64, 3, 256, 256], P(('grp', 'row')), parts along dimension 0, may hold values from 0 to 104857.6, as said below
- fields: float32 [16384], P(('grp', 'row')), parts along dimension 0, may hold values from -4 to 4
- field_first: float32 [16384], P(('grp', 'row')), parts along dimension 0, may hold values from -640 to 640
- field_second: float32 [16384], P(('grp', 'row')), parts along dimension 0, may hold values from 41943.04 to 2097152
Outputs:
- new_couplings: float32 [64, 3, 256, 256], P(('grp', 'row')), parts along dimension 0
- new_first: float32 [64, 3, 256, 256], P(('grp', 'row')), parts along dimension 0
- new_second: float32 [64, 3, 256, 256], P(('grp', 'row')), parts along dimension 0
- new_fields: float32 [16384], P(('grp', 'row')), parts along dimension 0
- new_field_first: float32 [16384], P(('grp', 'row')), parts along dimension 0
- new_field_second: float32 [16384], P(('grp', 'row')), parts along dimension 0
The draws below stay inside these ranges and needn't reach their ends.
There are 2 independent parts, one for each index of `grp`. The reference program is written for one: setup_inputs(seed, part) draws one part's arguments, and reference() takes and returns one part's arrays. A program takes and returns all parts, laid end to end along the dimension named above; each array names one. Nothing has to cross between parts.
Inputs may be any that keep to these rules, and one draw needn't show every extreme that they name: Entries are 0 or 1. Column 1 is always 1; pattern[b, 2] equals pattern[b + 1, 0]; pattern[0, 0] and pattern[31, 2] are 0. `frames`: 0 or 1. `couplings`: zero in every block whose pattern entry is 0 and on the diagonal of slot 1; slot 1 of each block row is symmetric; slot 0 of block row b is the transpose of slot 2 of block row b - 1. `first_moment`: same zeros and mirror structure as couplings. `second_moment`: same zeros and mirror structure as couplings; not negative.
All inputs are finite; a program needn't handle non-finite values.
Results may differ from the reference program's by a relative error of at most 0.0012.
Values may be sent and summed in bfloat16 or wider, within the bound.
A program may use at most 64 MiB of HBM per device.

```python
import math
import jax
import jax.numpy as jnp
from jax import lax

FRAMES = 2048
BLK = 256
STEPS = 2
PRIOR_STEPS = 100
NBLK = 32
NEURONS = 8192


def shared_links(key):
    link_key = jax.random.fold_in(key, 11)
    raw_draws = jax.random.randint(link_key, (NBLK,), 0, 10)
    link_flags = (raw_draws < 6).astype(jnp.int32)
    return link_flags * (jnp.arange(NBLK) < NBLK - 1).astype(jnp.int32)


def arrange_blocks(link_flags, linked, diagonal):
    upward = linked * link_flags.astype(jnp.float32)[:, None, None]
    zero_block = jnp.zeros((1, BLK, BLK), jnp.float32)
    downward = jnp.concatenate([zero_block, jnp.swapaxes(upward[:-1], 1, 2)], axis=0)
    return jnp.stack([downward, diagonal, upward], axis=1)


def symmetric_blocks(block_values, factor):
    off_diagonal = 1.0 - jnp.eye(BLK, dtype=jnp.float32)
    return (block_values + jnp.swapaxes(block_values, 1, 2)) * factor * off_diagonal


def draw_frames(key, part):
    key = jax.random.fold_in(key, 1)
    rate_key, spike_key = jax.random.split(key)
    fire_rates = jax.random.randint(rate_key, (NEURONS,), 40, 400)
    raw_draws = jax.random.randint(spike_key, (FRAMES, NEURONS), 0, 1000)
    return (raw_draws < fire_rates[None, :]).astype(jnp.float32).astype(jnp.bfloat16)


def draw_pattern(key, part):
    link_flags = shared_links(key)
    from_below = jnp.concatenate([jnp.zeros((1,), jnp.int32), link_flags[:-1]])
    return jnp.stack([from_below, jnp.ones_like(link_flags), link_flags], axis=1)


def draw_couplings(key, part):
    link_flags = shared_links(key)
    key = jax.random.fold_in(key, 2)
    normal_key, diag_key = jax.random.split(key)
    block_shape = (NBLK, BLK, BLK)
    linked = jnp.clip(0.1 * jax.random.normal(normal_key, block_shape, jnp.float32), -0.45, 0.45)
    diagonal = jnp.clip(0.1 * jax.random.normal(diag_key, block_shape, jnp.float32), -0.45, 0.45)
    return arrange_blocks(link_flags, linked, symmetric_blocks(diagonal, 0.7071))


def draw_first_moment(key, part):
    link_flags = shared_links(key)
    key = jax.random.fold_in(key, 3)
    normal_key, diag_key = jax.random.split(key)
    block_shape = (NBLK, BLK, BLK)
    bound_value = FRAMES / 10.0
    linked = jnp.clip(FRAMES / 40.0 * jax.random.normal(normal_key, block_shape, jnp.float32), -bound_value, bound_value)
    diagonal = jnp.clip(FRAMES / 40.0 * jax.random.normal(diag_key, block_shape, jnp.float32), -bound_value, bound_value)
    return arrange_blocks(link_flags, linked, symmetric_blocks(diagonal, 0.5))


def draw_second_moment(key, part):
    link_flags = shared_links(key)
    key = jax.random.fold_in(key, 4)
    normal_key, diag_key = jax.random.split(key)
    block_shape = (NBLK, BLK, BLK)
    low_log = jnp.log(FRAMES * FRAMES / 4000.0)
    high_log = jnp.log(FRAMES * FRAMES / 40.0)
    linked = jnp.exp(jax.random.uniform(normal_key, block_shape, jnp.float32, low_log, high_log))
    diagonal = jnp.exp(jax.random.uniform(diag_key, block_shape, jnp.float32, low_log, high_log))
    return arrange_blocks(link_flags, linked, symmetric_blocks(diagonal, 0.5))


def shard_levels(rng, dims, cuts, least, high):
    gain = 1.0
    for dim, blocks in cuts:
        steps = jax.random.uniform(jax.random.fold_in(jax.random.fold_in(rng, 6), dim), (blocks,), jnp.float32, least / len(cuts), high / len(cuts))
        gain = gain * jnp.repeat(jnp.exp(steps), dims[dim] // blocks).reshape((-1,) + (1,) * (len(dims) - 1 - dim))
    return gain


def bell_draw(stream_key, extent, scale, bound, shards=(), held_as=jnp.bfloat16):
    array = jax.random.normal(stream_key, extent, jnp.float32) * scale
    if len(shards) > 0:
        array = shard_levels(stream_key, extent, shards, -0.22, 0.18) * array
    return jnp.clip(array, min=-bound, max=bound).astype(held_as)


def setup_inputs(seed: int = 0, part: int = 0) -> dict:
    key_of = jax.random.split(jax.random.key(seed), 9)
    part_keys = jax.random.split(jax.random.fold_in(key_of[8], part), 9)
    return {
        "frames": draw_frames(jax.random.fold_in(jax.random.fold_in(key_of[8], part), 71), part),
        "pattern": draw_pattern(jax.random.fold_in(jax.random.fold_in(key_of[8], part), 71), part),
        "couplings": draw_couplings(jax.random.fold_in(jax.random.fold_in(key_of[8], part), 71), part),
        "first_moment": draw_first_moment(jax.random.fold_in(jax.random.fold_in(key_of[8], part), 71), part),
        "second_moment": draw_second_moment(jax.random.fold_in(jax.random.fold_in(key_of[8], part), 71), part),
        "fields": bell_draw(part_keys[5], (NEURONS,), 1.0, 4.0, ((0, 16),), jnp.float32),
        "field_first": bell_draw(part_keys[6], (NEURONS,), (FRAMES / 20), 640.0, ((0, 16),), jnp.float32),
        "field_second": jnp.clip(jnp.exp(math.log(2097152) - 3.912023 * jax.random.uniform(part_keys[7], (NEURONS,), jnp.float32) ** shard_levels(part_keys[7], (NEURONS,), ((0, 16),), -0.2, 0.2)), 41943.04, 2097152),
    }


BETA_ONE = 0.9
BETA_TWO = 0.999
LEARN_RATE = 0.02
EPSILON = 1e-08

def adam_update(parameter, first_moment, second_moment, gradient, step_count):
    first_moment = BETA_ONE * first_moment + (1.0 - BETA_ONE) * gradient
    second_moment = BETA_TWO * second_moment + (1.0 - BETA_TWO) * gradient * gradient
    first_hat = first_moment / (1.0 - BETA_ONE ** step_count)
    second_hat = second_moment / (1.0 - BETA_TWO ** step_count)
    parameter = parameter - LEARN_RATE * first_hat / (jnp.sqrt(second_hat) + EPSILON)
    return (parameter, first_moment, second_moment)

def reference(frames, pattern, couplings, first_moment, second_moment, fields, field_first, field_second):
    spikes = frames.reshape(FRAMES, NBLK, BLK).transpose(1, 0, 2)
    zero_frames = jnp.zeros((1, FRAMES, BLK), jnp.bfloat16)
    padded_spikes = jnp.concatenate([zero_frames, spikes, zero_frames], axis=0)
    spikes_float = spikes.astype(jnp.float32)
    occupied = pattern.astype(jnp.float32)
    all_ones = jnp.ones((BLK, BLK), jnp.float32)
    identity_matrix = jnp.eye(BLK, dtype=jnp.float32)
    slot_mask = occupied[:, :, None, None] * jnp.stack([all_ones, all_ones - identity_matrix, all_ones])[None]
    zero_weight = jnp.zeros((1, BLK, BLK), jnp.bfloat16)
    zero_half = jnp.zeros((1, BLK, BLK), jnp.float32)
    block_indices = jnp.arange(NBLK, dtype=jnp.int32)
    contract_frames = (((0,), (0,)), ((), ()))
    for step_index in range(STEPS):
        step_count = PRIOR_STEPS + step_index + 1
        weights = couplings.astype(jnp.bfloat16)
        lower_weights = jnp.concatenate([zero_weight, weights[:-1, 2]], axis=0)
        upper_weights = jnp.concatenate([weights[1:, 0], zero_weight], axis=0)

        def block_logits(block_index):
            own_term = jnp.dot(padded_spikes[block_index + 1], weights[block_index, 1], preferred_element_type=jnp.float32)
            below_term = jnp.dot(padded_spikes[block_index], lower_weights[block_index], preferred_element_type=jnp.float32)
            above_term = jnp.dot(padded_spikes[block_index + 2], upper_weights[block_index], preferred_element_type=jnp.float32)
            return own_term + below_term + above_term
        logit_terms = lax.map(block_logits, block_indices)
        logits = fields.reshape(NBLK, 1, BLK) + logit_terms
        deviation = jax.nn.sigmoid(logits) - spikes_float
        residual = deviation.astype(jnp.bfloat16)
        field_grad = lax.optimization_barrier(jnp.sum(deviation, axis=1)).reshape(NEURONS)
        padded_residual = jnp.concatenate([zero_frames, residual, zero_frames], axis=0)

        def block_halves(block_index):
            own_spikes = padded_spikes[block_index + 1]
            products = [lax.dot_general(own_spikes, padded_residual[block_index + offset], contract_frames, preferred_element_type=jnp.float32) for offset in range(3)]
            return jnp.stack(products)
        halves = lax.map(block_halves, block_indices)
        mirror_low = jnp.concatenate([zero_half, halves[:-1, 2]], axis=0)
        mirror_high = jnp.concatenate([halves[1:, 0], zero_half], axis=0)
        slot_low = halves[:, 0] + jnp.swapaxes(mirror_low, 1, 2)
        slot_mid = halves[:, 1] + jnp.swapaxes(halves[:, 1], 1, 2)
        slot_high = halves[:, 2] + jnp.swapaxes(mirror_high, 1, 2)
        gradient = jnp.stack([slot_low, slot_mid, slot_high], axis=1) * slot_mask
        couplings, first_moment, second_moment = adam_update(couplings, first_moment, second_moment, gradient, step_count)
        fields, field_first, field_second = adam_update(fields, field_first, field_second, field_grad, step_count)
    return (couplings, first_moment, second_moment, fields, field_first, field_second)
```

```python
import functools

import jax
import jax.numpy as jnp
from jax import lax
from jax.experimental import pallas as pl
from jax.experimental.pallas import tpu as pltpu
from jax.sharding import PartitionSpec as P

PRIOR_STEPS = 100
BETA_ONE = 0.9
BETA_TWO = 0.999
LEARN_RATE = 0.02
EPSILON = 1e-08
MESH = pl.DeviceIdType.MESH
PIECE = 256
SPAN = 512


def adam_update(parameter, first_moment, second_moment, gradient, step_count):
    first_moment = BETA_ONE * first_moment + (1.0 - BETA_ONE) * gradient
    second_moment = BETA_TWO * second_moment + (1.0 - BETA_TWO) * gradient * gradient
    first_rate = LEARN_RATE / (1.0 - BETA_ONE**step_count)
    second_hat = second_moment * (1.0 / (1.0 - BETA_TWO**step_count))
    parameter = parameter - first_rate * first_moment / (jnp.sqrt(second_hat) + EPSILON)
    return (parameter, first_moment, second_moment)


def dot(a, b):
    return jnp.dot(a, b, preferred_element_type=jnp.float32)


def dot_nt(a, b):
    return lax.dot_general(a, b, (((1,), (1,)), ((), ())), preferred_element_type=jnp.float32)


def kernel(
    count,
    frames_hbm, pattern, p_hbm, m_hbm, v_hbm, fields, field_first, field_second,
    p_out, m_out, v_out, grad_out, fields_out, field_first_out, field_second_out, field_grad_out,
    own, low, high, turned, p, m, v, w_own, w_low, w_high, half_low, half_high, field_sum,
    mirror_send, mirror_recv,
    halo_send_sem, halo_recv_sem, mirror_send_sem, mirror_recv_sem, own_sem, pmv_sem, out_sem,
):
    frame_count, width = low.shape
    pieces = frame_count // PIECE
    me = lax.axis_index("row")
    left = lax.rem(me + count - 1, count)
    right = lax.rem(me + 1, count)
    has_left = me > 0
    has_right = me < count - 1

    own_copy = pltpu.make_async_copy(frames_hbm, own, own_sem)
    pmv_copies = [
        pltpu.make_async_copy(src, dst, pmv_sem.at[k])
        for k, (src, dst) in enumerate(((p_hbm, p), (m_hbm, m), (v_hbm, v)))
    ]
    own_copy.start()
    for c in pmv_copies:
        c.start()

    def halo_copy(flow, i):
        rows = pl.ds(pl.multiple_of(i * PIECE, PIECE), PIECE)
        return pltpu.make_async_remote_copy(
            src_ref=frames_hbm.at[rows, pl.ds(flow * width, width)],
            dst_ref=(high, low)[flow].at[rows, :],
            send_sem=halo_send_sem.at[flow, i],
            recv_sem=halo_recv_sem.at[flow, i],
            device_id={"row": (left, right)[flow]},
            device_id_type=MESH,
        )

    def mirror_copy(step, flow):
        return pltpu.make_async_remote_copy(
            src_ref=mirror_send.at[step, flow],
            dst_ref=mirror_recv.at[step, flow],
            send_sem=mirror_send_sem.at[step, flow],
            recv_sem=mirror_recv_sem.at[step, flow],
            device_id={"row": (left, right)[flow]},
            device_id_type=MESH,
        )

    barrier = pltpu.get_barrier_semaphore()

    @pl.when(has_left)
    def _():
        pl.semaphore_signal(barrier, inc=1, device_id={"row": left}, device_id_type=MESH)

    @pl.when(has_right)
    def _():
        pl.semaphore_signal(barrier, inc=1, device_id={"row": right}, device_id_type=MESH)

    pl.semaphore_wait(barrier, has_left.astype(jnp.int32) + has_right.astype(jnp.int32))

    @pl.loop(0, pieces)
    def _(i):
        @pl.when(has_left)
        def _():
            halo_copy(0, i).start()

        @pl.when(has_right)
        def _():
            halo_copy(1, i).start()

    @pl.when(jnp.logical_not(has_left))
    def _():
        low[...] = jnp.zeros_like(low)
        for step in range(2):
            mirror_recv[step, 1] = jnp.zeros((width, width), jnp.bfloat16)

    @pl.when(jnp.logical_not(has_right))
    def _():
        high[...] = jnp.zeros_like(high)
        for step in range(2):
            mirror_recv[step, 0] = jnp.zeros((width, width), jnp.bfloat16)

    diagonal = lax.broadcasted_iota(jnp.int32, (width, width), 0) == lax.broadcasted_iota(
        jnp.int32, (width, width), 1
    )

    def set_weights(b, s, value):
        value = value.astype(jnp.bfloat16)
        if (b, s) == (0, 0):
            w_low[...] = value
        elif (b, s) == (1, 2):
            w_high[...] = value
        else:
            c = b + s - 1
            w_own[b * width:(b + 1) * width, c * width:(c + 1) * width] = value

    pmv_copies[0].wait()
    for b in range(2):
        for s in range(3):
            set_weights(b, s, p[b, s])
    own_copy.wait()

    def run_pass(rows, size, fields_row, turn):
        x_own, x_low, x_high = own[rows, :], low[rows, :], high[rows, :]
        if turn:
            turned[:width, rows] = x_low.T
            turned[width:3 * width, rows] = x_own.T
            turned[3 * width:, rows] = x_high.T
        inner = dot(x_own, w_own[...])
        outer = jnp.concatenate([dot_nt(x_low, w_low[...]), dot_nt(x_high, w_high[...])], axis=1)
        logits = inner + outer + fields_row
        deviation = 0.5 * jnp.tanh(0.5 * logits) + (0.5 - x_own.astype(jnp.float32))
        field_sum[...] += jnp.sum(deviation.reshape(size // 8, 8, 2 * width), axis=0)
        residual = deviation.astype(jnp.bfloat16)
        half_low[...] += dot(turned[:3 * width, rows], residual[:, :width])
        half_high[...] += dot(turned[width:, rows], residual[:, width:])

    def gradient_of(step, b, s):
        if (b, s) == (0, 0):
            value = half_low[:width, :].T + mirror_recv[step, 1].astype(jnp.float32)
        elif (b, s) == (1, 2):
            value = half_high[2 * width:, :].T + mirror_recv[step, 0].astype(jnp.float32)
        elif s == 1:
            half = half_low[width:2 * width, :] if b == 0 else half_high[width:2 * width, :]
            value = jnp.where(diagonal, 0.0, half + half.T)
        elif b == 0:
            value = half_high[:width, :] + half_low[2 * width:, :].T
        else:
            value = half_low[2 * width:, :] + half_high[:width, :].T
        return value * pattern[b, s].astype(jnp.float32)

    for step in range(2):
        half_low[...] = jnp.zeros_like(half_low)
        half_high[...] = jnp.zeros_like(half_high)
        field_sum[...] = jnp.zeros_like(field_sum)
        if step == 0:
            @pl.loop(0, pieces)
            def _(i):
                @pl.when(has_left)
                def _():
                    halo_copy(1, i).wait_recv()

                @pl.when(has_right)
                def _():
                    halo_copy(0, i).wait_recv()

                run_pass(pl.ds(pl.multiple_of(i * PIECE, PIECE), PIECE), PIECE, fields[...], True)
        else:
            @pl.loop(0, frame_count // SPAN)
            def _(i):
                run_pass(pl.ds(pl.multiple_of(i * SPAN, SPAN), SPAN), SPAN, fields_out[...], False)

        mirror_send[step, 0] = half_low[:width, :].astype(jnp.bfloat16)
        mirror_send[step, 1] = half_high[2 * width:, :].astype(jnp.bfloat16)

        @pl.when(has_left)
        def _():
            mirror_copy(step, 0).start()

        @pl.when(has_right)
        def _():
            mirror_copy(step, 1).start()

        field_grad = jnp.sum(field_sum[...], axis=0, keepdims=True)
        if step == 0:
            fields_out[...], field_first_out[...], field_second_out[...] = adam_update(
                fields[...], field_first[...], field_second[...], field_grad, PRIOR_STEPS + 1
            )
            pmv_copies[1].wait()
            pmv_copies[2].wait()
        else:
            field_grad_out[...] = field_grad

        for b, s in ((0, 1), (0, 2), (1, 0), (1, 1), (0, 0), (1, 2)):
            if (b, s) == (0, 0):
                @pl.when(has_left)
                def _():
                    mirror_copy(step, 1).wait_recv()
            elif (b, s) == (1, 2):
                @pl.when(has_right)
                def _():
                    mirror_copy(step, 0).wait_recv()
            gradient = gradient_of(step, b, s)
            if step == 0:
                p[b, s], m[b, s], v[b, s] = adam_update(
                    p[b, s], m[b, s], v[b, s], gradient, PRIOR_STEPS + 1
                )
                set_weights(b, s, p[b, s])
            else:
                grad_out[b, s] = gradient
        if step == 0:
            out_copies = [
                pltpu.make_async_copy(src, dst, out_sem.at[k])
                for k, (src, dst) in enumerate(((p, p_out), (m, m_out), (v, v_out)))
            ]
            for c in out_copies:
                c.start()

    for c in out_copies:
        c.wait()

    @pl.when(has_left)
    def _():
        for step in range(2):
            mirror_copy(step, 0).wait_send()

    @pl.when(has_right)
    def _():
        for step in range(2):
            mirror_copy(step, 1).wait_send()

    @pl.loop(0, pieces)
    def _(i):
        @pl.when(has_left)
        def _():
            halo_copy(0, i).wait_send()

        @pl.when(has_right)
        def _():
            halo_copy(1, i).wait_send()


def on_device(
    count, frames, pattern, couplings, first_moment, second_moment, fields, field_first, field_second
):
    frame_count, neurons = frames.shape
    width = couplings.shape[-1]
    blocks = jax.ShapeDtypeStruct(couplings.shape, jnp.float32)
    row = jax.ShapeDtypeStruct((1, neurons), jnp.float32)
    vmem = pl.BlockSpec(memory_space=pltpu.VMEM)
    anywhere = pl.BlockSpec(memory_space=pl.ANY)
    pieces = frame_count // PIECE
    p, m, v, gradient, f, ff, fs, field_grad = pl.pallas_call(
        functools.partial(kernel, count),
        out_shape=[blocks, blocks, blocks, blocks, row, row, row, row],
        in_specs=[anywhere, pl.BlockSpec(memory_space=pltpu.SMEM)] + [anywhere] * 3 + [vmem] * 3,
        out_specs=[anywhere] * 3 + [vmem] * 5,
        scratch_shapes=[
            pltpu.VMEM((frame_count, neurons), jnp.bfloat16),
            pltpu.VMEM((frame_count, width), jnp.bfloat16),
            pltpu.VMEM((frame_count, width), jnp.bfloat16),
            pltpu.VMEM((4 * width, frame_count), jnp.bfloat16),
            pltpu.VMEM(couplings.shape, jnp.float32),
            pltpu.VMEM(couplings.shape, jnp.float32),
            pltpu.VMEM(couplings.shape, jnp.float32),
            pltpu.VMEM((neurons, neurons), jnp.bfloat16),
            pltpu.VMEM((width, width), jnp.bfloat16),
            pltpu.VMEM((width, width), jnp.bfloat16),
            pltpu.VMEM((3 * width, width), jnp.float32),
            pltpu.VMEM((3 * width, width), jnp.float32),
            pltpu.VMEM((8, neurons), jnp.float32),
            pltpu.VMEM((2, 2, width, width), jnp.bfloat16),
            pltpu.VMEM((2, 2, width, width), jnp.bfloat16),
            pltpu.SemaphoreType.DMA((2, pieces)),
            pltpu.SemaphoreType.DMA((2, pieces)),
            pltpu.SemaphoreType.DMA((2, 2)),
            pltpu.SemaphoreType.DMA((2, 2)),
            pltpu.SemaphoreType.DMA,
            pltpu.SemaphoreType.DMA((3,)),
            pltpu.SemaphoreType.DMA((3,)),
        ],
        compiler_params=pltpu.CompilerParams(
            collective_id=0, has_side_effects=True, vmem_limit_bytes=48 * 1024 * 1024
        ),
    )(
        frames, pattern, couplings, first_moment, second_moment,
        fields.reshape(1, neurons), field_first.reshape(1, neurons), field_second.reshape(1, neurons),
    )
    p, m, v = adam_update(p, m, v, gradient, PRIOR_STEPS + 2)
    f, ff, fs = adam_update(
        f.reshape(neurons), ff.reshape(neurons), fs.reshape(neurons),
        field_grad.reshape(neurons), PRIOR_STEPS + 2,
    )
    return (p, m, v, f, ff, fs)


def solution(mesh):
    blocks = P(("grp", "row"), None, None, None)
    vector = P(("grp", "row"))
    return jax.shard_map(
        functools.partial(on_device, mesh.shape["row"]),
        mesh=mesh,
        in_specs=(P("grp", "row"), P(("grp", "row"), None)) + (blocks,) * 3 + (vector,) * 3,
        out_specs=(blocks,) * 3 + (vector,) * 3,
        check_vma=False,
    )
```

```python
import functools

import jax
import jax.numpy as jnp
from jax import lax
from jax.experimental import pallas as pl
from jax.experimental.pallas import tpu as pltpu
from jax.sharding import PartitionSpec as P

PRIOR_STEPS = 100
BETA_ONE = 0.9
BETA_TWO = 0.999
LEARN_RATE = 0.02
EPSILON = 1e-08
MESH = pl.DeviceIdType.MESH
PIECE = 256
SPAN = 512


def adam_update(parameter, first_moment, second_moment, gradient, step_count):
    first_moment = BETA_ONE * first_moment + (1.0 - BETA_ONE) * gradient
    second_moment = BETA_TWO * second_moment + (1.0 - BETA_TWO) * gradient * gradient
    first_rate = LEARN_RATE / (1.0 - BETA_ONE**step_count)
    second_hat = second_moment * (1.0 / (1.0 - BETA_TWO**step_count))
    parameter = parameter - first_rate * first_moment / (jnp.sqrt(second_hat) + EPSILON)
    return (parameter, first_moment, second_moment)


def dot(a, b):
    return jnp.dot(a, b, preferred_element_type=jnp.float32)


def dot_nt(a, b):
    return lax.dot_general(a, b, (((1,), (1,)), ((), ())), preferred_element_type=jnp.float32)


def kernel(
    count,
    frames_hbm, p_hbm, m_hbm, v_hbm, vectors, p_out, m_out, v_out, vectors_out,
    own, low, high, turned, residuals, p, m, v, w_own, w_low, w_high, half_low, half_high, local,
    field_sum, fields, mirror_send, mirror_recv,
    halo_send_sem, halo_recv_sem, mirror_send_sem, mirror_recv_sem, own_sem, load_sem, out_sem,
):
    frame_count, width = low.shape
    pieces = frame_count // PIECE
    me = lax.axis_index("row")
    left = lax.rem(me + count - 1, count)
    right = lax.rem(me + 1, count)
    has_left = me > 0
    has_right = me < count - 1

    own_copy = pltpu.make_async_copy(frames_hbm, own, own_sem)
    loads = [
        pltpu.make_async_copy(src, dst, load_sem.at[k])
        for k, (src, dst) in enumerate(((p_hbm, p), (m_hbm, m), (v_hbm, v)))
    ]
    own_copy.start()
    for c in loads:
        c.start()

    def halo_copy(flow, i):
        rows = pl.ds(pl.multiple_of(i * PIECE, PIECE), PIECE)
        return pltpu.make_async_remote_copy(
            src_ref=frames_hbm.at[rows, pl.ds(flow * width, width)],
            dst_ref=(high, low)[flow].at[rows, :],
            send_sem=halo_send_sem.at[flow, i],
            recv_sem=halo_recv_sem.at[flow, i],
            device_id={"row": (left, right)[flow]},
            device_id_type=MESH,
        )

    def mirror_copy(step, flow):
        return pltpu.make_async_remote_copy(
            src_ref=mirror_send.at[step, flow],
            dst_ref=mirror_recv.at[step, flow],
            send_sem=mirror_send_sem.at[step, flow],
            recv_sem=mirror_recv_sem.at[step, flow],
            device_id={"row": (left, right)[flow]},
            device_id_type=MESH,
        )

    barrier = pltpu.get_barrier_semaphore()

    @pl.when(has_left)
    def _():
        pl.semaphore_signal(barrier, inc=1, device_id={"row": left}, device_id_type=MESH)

    @pl.when(has_right)
    def _():
        pl.semaphore_signal(barrier, inc=1, device_id={"row": right}, device_id_type=MESH)

    pl.semaphore_wait(barrier, has_left.astype(jnp.int32) + has_right.astype(jnp.int32))

    @pl.loop(0, pieces)
    def _(i):
        @pl.when(has_left)
        def _():
            halo_copy(0, i).start()

        @pl.when(has_right)
        def _():
            halo_copy(1, i).start()

    @pl.when(jnp.logical_not(has_left))
    def _():
        low[...] = jnp.zeros_like(low)
        for step in range(2):
            mirror_recv[step, 1] = jnp.zeros((width, width), jnp.bfloat16)

    @pl.when(jnp.logical_not(has_right))
    def _():
        high[...] = jnp.zeros_like(high)
        for step in range(2):
            mirror_recv[step, 0] = jnp.zeros((width, width), jnp.bfloat16)

    diagonal = lax.broadcasted_iota(jnp.int32, (width, width), 0) == lax.broadcasted_iota(
        jnp.int32, (width, width), 1
    )

    def set_weights(b, s, value):
        value = value.astype(jnp.bfloat16)
        if (b, s) == (0, 0):
            w_low[...] = value
        elif (b, s) == (1, 2):
            w_high[...] = value
        else:
            c = b + s - 1
            w_own[b * width:(b + 1) * width, c * width:(c + 1) * width] = value

    fields[...] = vectors[:1, :]
    loads[0].wait()
    for b in range(2):
        for s in range(3):
            set_weights(b, s, p[b, s])
    own_copy.wait()

    def run_pass(rows, size, turn):
        x_own, x_low, x_high = own[rows, :], low[rows, :], high[rows, :]
        if turn:
            turned[:width, rows] = x_low.T
            turned[width:3 * width, rows] = x_own.T
            turned[3 * width:, rows] = x_high.T
        inner = dot(x_own, w_own[...])
        outer = jnp.concatenate([dot_nt(x_low, w_low[...]), dot_nt(x_high, w_high[...])], axis=1)
        logits = inner + outer + fields[...]
        deviation = 0.5 * jnp.tanh(0.5 * logits) + (0.5 - x_own.astype(jnp.float32))
        field_sum[...] += jnp.sum(deviation.reshape(size // 8, 8, 2 * width), axis=0)
        residual = deviation.astype(jnp.bfloat16)
        residuals[rows, :] = residual
        half_low[...] += dot(turned[:width, rows], residual[:, :width])
        half_high[...] += dot(turned[3 * width:, rows], residual[:, width:])

    def gradient_of(step, b, s):
        if (b, s) == (0, 0):
            value = half_low[...].T + mirror_recv[step, 1].astype(jnp.float32)
        elif (b, s) == (1, 2):
            value = half_high[...].T + mirror_recv[step, 0].astype(jnp.float32)
        else:
            one = slice(b * width, (b + 1) * width)
            two = slice((b + s - 1) * width, (b + s) * width)
            value = local[one, two] + local[two, one].T
            if s == 1:
                value = jnp.where(diagonal, 0.0, value)
        slot = 3 * b + s
        return value * vectors[3:4, slot:slot + 1]

    out_copies = []
    for step in range(2):
        half_low[...] = jnp.zeros_like(half_low)
        half_high[...] = jnp.zeros_like(half_high)
        field_sum[...] = jnp.zeros_like(field_sum)
        if step == 0:
            @pl.loop(0, pieces)
            def _(i):
                @pl.when(has_left)
                def _():
                    halo_copy(1, i).wait_recv()

                @pl.when(has_right)
                def _():
                    halo_copy(0, i).wait_recv()

                run_pass(pl.ds(pl.multiple_of(i * PIECE, PIECE), PIECE), PIECE, True)
        else:
            @pl.loop(0, frame_count // SPAN)
            def _(i):
                run_pass(pl.ds(pl.multiple_of(i * SPAN, SPAN), SPAN), SPAN, False)

        mirror_send[step, 0] = half_low[...].astype(jnp.bfloat16)
        mirror_send[step, 1] = half_high[...].astype(jnp.bfloat16)

        @pl.when(has_left)
        def _():
            mirror_copy(step, 0).start()

        @pl.when(has_right)
        def _():
            mirror_copy(step, 1).start()

        if step == 0:
            for c in loads[1:]:
                c.wait()
        field_grad = jnp.sum(field_sum[...], axis=0, keepdims=True)
        if step == 0:
            fields[...], vectors_out[1:2, :], vectors_out[2:3, :] = adam_update(
                fields[...], vectors[1:2, :], vectors[2:3, :], field_grad, PRIOR_STEPS + 1
            )
            vectors_out[:1, :] = fields[...]
        else:
            vectors_out[3:4, :] = field_grad
        local[...] = dot(turned[width:3 * width, :], residuals[...])

        for b, s in ((0, 1), (0, 2), (1, 0), (1, 1), (0, 0), (1, 2)):
            if (b, s) == (0, 0):
                @pl.when(has_left)
                def _():
                    mirror_copy(step, 1).wait_recv()
            elif (b, s) == (1, 2):
                @pl.when(has_right)
                def _():
                    mirror_copy(step, 0).wait_recv()
            p[b, s], m[b, s], v[b, s] = adam_update(
                p[b, s], m[b, s], v[b, s], gradient_of(step, b, s), PRIOR_STEPS + 1 + step
            )
            if step == 0:
                set_weights(b, s, p[b, s])
            else:
                for k, (src, dst) in enumerate(((p, p_out), (m, m_out), (v, v_out))):
                    copy = pltpu.make_async_copy(src.at[b, s], dst.at[b, s], out_sem.at[k, 3 * b + s])
                    copy.start()
                    out_copies.append(copy)

    for c in out_copies:
        c.wait()

    @pl.when(has_left)
    def _():
        for step in range(2):
            mirror_copy(step, 0).wait_send()

    @pl.when(has_right)
    def _():
        for step in range(2):
            mirror_copy(step, 1).wait_send()

    @pl.loop(0, pieces)
    def _(i):
        @pl.when(has_left)
        def _():
            halo_copy(0, i).wait_send()

        @pl.when(has_right)
        def _():
            halo_copy(1, i).wait_send()


def on_device(
    count, frames, pattern, couplings, first_moment, second_moment, fields, field_first, field_second
):
    frame_count, neurons = frames.shape
    width = couplings.shape[-1]
    blocks = jax.ShapeDtypeStruct(couplings.shape, jnp.float32)
    rows = jax.ShapeDtypeStruct((4, neurons), jnp.float32)
    vmem = pl.BlockSpec(memory_space=pltpu.VMEM)
    anywhere = pl.BlockSpec(memory_space=pl.ANY)
    pieces = frame_count // PIECE
    vectors = jnp.stack(
        [
            fields, field_first, field_second,
            jnp.pad(pattern.reshape(-1).astype(jnp.float32), (0, neurons - pattern.size)),
        ]
    )
    p, m, v, vectors = pl.pallas_call(
        functools.partial(kernel, count),
        out_shape=[blocks, blocks, blocks, rows],
        in_specs=[anywhere] * 4 + [vmem],
        out_specs=[anywhere] * 3 + [vmem],
        scratch_shapes=[
            pltpu.VMEM((frame_count, neurons), jnp.bfloat16),
            pltpu.VMEM((frame_count, width), jnp.bfloat16),
            pltpu.VMEM((frame_count, width), jnp.bfloat16),
            pltpu.VMEM((4 * width, frame_count), jnp.bfloat16),
            pltpu.VMEM((frame_count, neurons), jnp.bfloat16),
            pltpu.VMEM(couplings.shape, jnp.float32),
            pltpu.VMEM(couplings.shape, jnp.float32),
            pltpu.VMEM(couplings.shape, jnp.float32),
            pltpu.VMEM((neurons, neurons), jnp.bfloat16),
            pltpu.VMEM((width, width), jnp.bfloat16),
            pltpu.VMEM((width, width), jnp.bfloat16),
            pltpu.VMEM((width, width), jnp.float32),
            pltpu.VMEM((width, width), jnp.float32),
            pltpu.VMEM((neurons, neurons), jnp.float32),
            pltpu.VMEM((8, neurons), jnp.float32),
            pltpu.VMEM((1, neurons), jnp.float32),
            pltpu.VMEM((2, 2, width, width), jnp.bfloat16),
            pltpu.VMEM((2, 2, width, width), jnp.bfloat16),
            pltpu.SemaphoreType.DMA((2, pieces)),
            pltpu.SemaphoreType.DMA((2, pieces)),
            pltpu.SemaphoreType.DMA((2, 2)),
            pltpu.SemaphoreType.DMA((2, 2)),
            pltpu.SemaphoreType.DMA,
            pltpu.SemaphoreType.DMA((3,)),
            pltpu.SemaphoreType.DMA((3, 6)),
        ],
        compiler_params=pltpu.CompilerParams(
            collective_id=0, has_side_effects=True, vmem_limit_bytes=48 * 1024 * 1024
        ),
    )(
        frames, couplings, first_moment, second_moment, vectors
    )
    f, ff, fs = adam_update(vectors[0], vectors[1], vectors[2], vectors[3], PRIOR_STEPS + 2)
    return (p, m, v, f, ff, fs)


def solution(mesh):
    blocks = P(("grp", "row"), None, None, None)
    vector = P(("grp", "row"))
    return jax.shard_map(
        functools.partial(on_device, mesh.shape["row"]),
        mesh=mesh,
        in_specs=(P("grp", "row"), P(("grp", "row"), None)) + (blocks,) * 3 + (vector,) * 3,
        out_specs=(blocks,) * 3 + (vector,) * 3,
        check_vma=False,
    )
```

```python
import functools

import jax
import jax.numpy as jnp
from jax import lax
from jax.experimental import pallas as pl
from jax.experimental.pallas import tpu as pltpu
from jax.sharding import PartitionSpec as P

PRIOR_STEPS = 100
BETA_ONE = 0.9
BETA_TWO = 0.999
LEARN_RATE = 0.02
EPSILON = 1e-08
MESH = pl.DeviceIdType.MESH
PIECE = 256
SPAN = 512


def adam_update(parameter, first_moment, second_moment, gradient, step_count):
    first_moment = BETA_ONE * first_moment + (1.0 - BETA_ONE) * gradient
    second_moment = BETA_TWO * second_moment + (1.0 - BETA_TWO) * gradient * gradient
    first_rate = LEARN_RATE / (1.0 - BETA_ONE**step_count)
    second_hat = second_moment * (1.0 / (1.0 - BETA_TWO**step_count))
    parameter = parameter - first_rate * first_moment / (jnp.sqrt(second_hat) + EPSILON)
    return (parameter, first_moment, second_moment)


def dot(a, b):
    return jnp.dot(a, b, preferred_element_type=jnp.float32)


def dot_nt(a, b):
    return lax.dot_general(a, b, (((1,), (1,)), ((), ())), preferred_element_type=jnp.float32)


def kernel(
    count,
    frames_hbm, p_hbm, m_hbm, v_hbm, vectors, p_out, m_out, v_out, vectors_out,
    own, low, high, turned, residuals, p, m, v, w_own, w_low, w_high, half_low, half_high, local,
    field_sum, fields, mirror_send, mirror_recv,
    halo_send_sem, halo_recv_sem, mirror_send_sem, mirror_recv_sem, own_sem, load_sem, out_sem,
):
    frame_count, width = low.shape
    pieces = frame_count // PIECE
    me = lax.axis_index("row")
    left = lax.rem(me + count - 1, count)
    right = lax.rem(me + 1, count)
    has_left = me > 0
    has_right = me < count - 1

    own_copy = pltpu.make_async_copy(frames_hbm, own, own_sem)
    loads = [
        pltpu.make_async_copy(src, dst, load_sem.at[k])
        for k, (src, dst) in enumerate(((p_hbm, p), (m_hbm, m), (v_hbm, v)))
    ]
    own_copy.start()
    for c in loads:
        c.start()

    def halo_copy(flow, i):
        rows = pl.ds(pl.multiple_of(i * PIECE, PIECE), PIECE)
        return pltpu.make_async_remote_copy(
            src_ref=frames_hbm.at[rows, pl.ds(flow * width, width)],
            dst_ref=(high, low)[flow].at[rows, :],
            send_sem=halo_send_sem.at[flow, i],
            recv_sem=halo_recv_sem.at[flow, i],
            device_id={"row": (left, right)[flow]},
            device_id_type=MESH,
        )

    def mirror_copy(step, flow):
        return pltpu.make_async_remote_copy(
            src_ref=mirror_send.at[step, flow],
            dst_ref=mirror_recv.at[step, flow],
            send_sem=mirror_send_sem.at[step, flow],
            recv_sem=mirror_recv_sem.at[step, flow],
            device_id={"row": (left, right)[flow]},
            device_id_type=MESH,
        )

    barrier = pltpu.get_barrier_semaphore()

    @pl.when(has_left)
    def _():
        pl.semaphore_signal(barrier, inc=1, device_id={"row": left}, device_id_type=MESH)

    @pl.when(has_right)
    def _():
        pl.semaphore_signal(barrier, inc=1, device_id={"row": right}, device_id_type=MESH)

    pl.semaphore_wait(barrier, has_left.astype(jnp.int32) + has_right.astype(jnp.int32))

    @pl.loop(0, pieces)
    def _(i):
        @pl.when(has_left)
        def _():
            halo_copy(0, i).start()

        @pl.when(has_right)
        def _():
            halo_copy(1, i).start()

    @pl.when(jnp.logical_not(has_left))
    def _():
        low[...] = jnp.zeros_like(low)
        for step in range(2):
            mirror_recv[step, 1] = jnp.zeros((width, width), jnp.bfloat16)

    @pl.when(jnp.logical_not(has_right))
    def _():
        high[...] = jnp.zeros_like(high)
        for step in range(2):
            mirror_recv[step, 0] = jnp.zeros((width, width), jnp.bfloat16)

    diagonal = lax.broadcasted_iota(jnp.int32, (width, width), 0) == lax.broadcasted_iota(
        jnp.int32, (width, width), 1
    )

    def set_weights(b, s, value):
        value = value.astype(jnp.bfloat16)
        if (b, s) == (0, 0):
            w_low[...] = value
        elif (b, s) == (1, 2):
            w_high[...] = value
        else:
            c = b + s - 1
            w_own[b * width:(b + 1) * width, c * width:(c + 1) * width] = value

    fields[...] = vectors[:1, :]
    loads[0].wait()
    for b in range(2):
        for s in range(3):
            set_weights(b, s, p[b, s])
    own_copy.wait()

    def run_pass(rows, size, turn):
        x_own, x_low, x_high = own[rows, :], low[rows, :], high[rows, :]
        if turn:
            turned[:width, rows] = x_low.T
            turned[width:3 * width, rows] = x_own.T
            turned[3 * width:, rows] = x_high.T
        inner = dot(x_own, w_own[...])
        outer = jnp.concatenate([dot_nt(x_low, w_low[...]), dot_nt(x_high, w_high[...])], axis=1)
        logits = inner + outer + fields[...]
        deviation = 0.5 * jnp.tanh(0.5 * logits) + (0.5 - x_own.astype(jnp.float32))
        field_sum[...] += jnp.sum(deviation.reshape(size // 8, 8, 2 * width), axis=0)
        residual = deviation.astype(jnp.bfloat16)
        residuals[rows, :] = residual
        half_low[...] += dot(turned[:width, rows], residual[:, :width])
        half_high[...] += dot(turned[3 * width:, rows], residual[:, width:])

    def gradient_of(step, b, s):
        if (b, s) == (0, 0):
            value = half_low[...].T + mirror_recv[step, 1].astype(jnp.float32)
        elif (b, s) == (1, 2):
            value = half_high[...].T + mirror_recv[step, 0].astype(jnp.float32)
        else:
            one = slice(b * width, (b + 1) * width)
            two = slice((b + s - 1) * width, (b + s) * width)
            value = local[one, two] + local[two, one].T
            if s == 1:
                value = jnp.where(diagonal, 0.0, value)
        return value * vectors[3 + b:4 + b, s:s + 1]

    out_copies = []
    for step in range(2):
        half_low[...] = jnp.zeros_like(half_low)
        half_high[...] = jnp.zeros_like(half_high)
        field_sum[...] = jnp.zeros_like(field_sum)
        if step == 0:
            @pl.loop(0, pieces)
            def _(i):
                @pl.when(has_left)
                def _():
                    halo_copy(1, i).wait_recv()

                @pl.when(has_right)
                def _():
                    halo_copy(0, i).wait_recv()

                run_pass(pl.ds(pl.multiple_of(i * PIECE, PIECE), PIECE), PIECE, True)
        else:
            @pl.loop(0, frame_count // SPAN)
            def _(i):
                run_pass(pl.ds(pl.multiple_of(i * SPAN, SPAN), SPAN), SPAN, False)

        mirror_send[step, 0] = half_low[...].astype(jnp.bfloat16)
        mirror_send[step, 1] = half_high[...].astype(jnp.bfloat16)

        @pl.when(has_left)
        def _():
            mirror_copy(step, 0).start()

        @pl.when(has_right)
        def _():
            mirror_copy(step, 1).start()

        if step == 0:
            for c in loads[1:]:
                c.wait()
        field_grad = jnp.sum(field_sum[...], axis=0, keepdims=True)
        if step == 0:
            fields[...], vectors_out[1:2, :], vectors_out[2:3, :] = adam_update(
                fields[...], vectors[1:2, :], vectors[2:3, :], field_grad, PRIOR_STEPS + 1
            )
            vectors_out[:1, :] = fields[...]
        else:
            vectors_out[3:4, :] = field_grad
        local[...] = dot(turned[width:3 * width, :], residuals[...])

        for b, s in ((0, 1), (0, 2), (1, 0), (1, 1), (0, 0), (1, 2)):
            if (b, s) == (0, 0):
                @pl.when(has_left)
                def _():
                    mirror_copy(step, 1).wait_recv()
            elif (b, s) == (1, 2):
                @pl.when(has_right)
                def _():
                    mirror_copy(step, 0).wait_recv()
            p[b, s], m[b, s], v[b, s] = adam_update(
                p[b, s], m[b, s], v[b, s], gradient_of(step, b, s), PRIOR_STEPS + 1 + step
            )
            if step == 0:
                set_weights(b, s, p[b, s])
            else:
                for k, (src, dst) in enumerate(((p, p_out), (m, m_out), (v, v_out))):
                    copy = pltpu.make_async_copy(src.at[b, s], dst.at[b, s], out_sem.at[k, 3 * b + s])
                    copy.start()
                    out_copies.append(copy)

    for c in out_copies:
        c.wait()

    @pl.when(has_left)
    def _():
        for step in range(2):
            mirror_copy(step, 0).wait_send()

    @pl.when(has_right)
    def _():
        for step in range(2):
            mirror_copy(step, 1).wait_send()

    @pl.loop(0, pieces)
    def _(i):
        @pl.when(has_left)
        def _():
            halo_copy(0, i).wait_send()

        @pl.when(has_right)
        def _():
            halo_copy(1, i).wait_send()


def store_kernel(p, m, v, p_out, m_out, v_out, sem):
    copies = [
        pltpu.make_async_copy(src.at[b], dst.at[b], sem.at[k, b])
        for k, (src, dst) in enumerate(((p, p_out), (m, m_out), (v, v_out)))
        for b in range(2)
    ]
    for c in copies:
        c.start()
    for c in copies:
        c.wait()


def on_device(
    count, frames, pattern, couplings, first_moment, second_moment, fields, field_first, field_second
):
    frame_count, neurons = frames.shape
    width = couplings.shape[-1]
    blocks = jax.ShapeDtypeStruct(couplings.shape, jnp.float32)
    rows = jax.ShapeDtypeStruct((4, neurons), jnp.float32)
    vmem = pl.BlockSpec(memory_space=pltpu.VMEM)
    anywhere = pl.BlockSpec(memory_space=pl.ANY)
    pieces = frame_count // PIECE
    vectors = jnp.concatenate(
        [
            fields[None], field_first[None], field_second[None],
            jnp.pad(pattern.astype(jnp.float32), ((0, 0), (0, neurons - pattern.shape[1]))),
        ]
    )
    p, m, v, vectors = pl.pallas_call(
        functools.partial(kernel, count),
        out_shape=[blocks, blocks, blocks, rows],
        in_specs=[anywhere] * 4 + [vmem],
        out_specs=[anywhere] * 3 + [vmem],
        scratch_shapes=[
            pltpu.VMEM((frame_count, neurons), jnp.bfloat16),
            pltpu.VMEM((frame_count, width), jnp.bfloat16),
            pltpu.VMEM((frame_count, width), jnp.bfloat16),
            pltpu.VMEM((4 * width, frame_count), jnp.bfloat16),
            pltpu.VMEM((frame_count, neurons), jnp.bfloat16),
            pltpu.VMEM(couplings.shape, jnp.float32),
            pltpu.VMEM(couplings.shape, jnp.float32),
            pltpu.VMEM(couplings.shape, jnp.float32),
            pltpu.VMEM((neurons, neurons), jnp.bfloat16),
            pltpu.VMEM((width, width), jnp.bfloat16),
            pltpu.VMEM((width, width), jnp.bfloat16),
            pltpu.VMEM((width, width), jnp.float32),
            pltpu.VMEM((width, width), jnp.float32),
            pltpu.VMEM((neurons, neurons), jnp.float32),
            pltpu.VMEM((8, neurons), jnp.float32),
            pltpu.VMEM((1, neurons), jnp.float32),
            pltpu.VMEM((2, 2, width, width), jnp.bfloat16),
            pltpu.VMEM((2, 2, width, width), jnp.bfloat16),
            pltpu.SemaphoreType.DMA((2, pieces)),
            pltpu.SemaphoreType.DMA((2, pieces)),
            pltpu.SemaphoreType.DMA((2, 2)),
            pltpu.SemaphoreType.DMA((2, 2)),
            pltpu.SemaphoreType.DMA,
            pltpu.SemaphoreType.DMA((3,)),
            pltpu.SemaphoreType.DMA((3, 6)),
        ],
        compiler_params=pltpu.CompilerParams(
            collective_id=0, has_side_effects=True, vmem_limit_bytes=48 * 1024 * 1024
        ),
    )(
        frames, couplings, first_moment, second_moment, vectors
    )
    p, m, v = pl.pallas_call(
        store_kernel,
        out_shape=[blocks] * 3,
        in_specs=[anywhere] * 3,
        out_specs=[anywhere] * 3,
        scratch_shapes=[pltpu.SemaphoreType.DMA((3, 2))],
    )(p, m, v)
    f, ff, fs = adam_update(vectors[0], vectors[1], vectors[2], vectors[3], PRIOR_STEPS + 2)
    return (p, m, v, f, ff, fs)


def solution(mesh):
    blocks = P(("grp", "row"), None, None, None)
    vector = P(("grp", "row"))
    return jax.shard_map(
        functools.partial(on_device, mesh.shape["row"]),
        mesh=mesh,
        in_specs=(P("grp", "row"), P(("grp", "row"), None)) + (blocks,) * 3 + (vector,) * 3,
        out_specs=(blocks,) * 3 + (vector,) * 3,
        check_vma=False,
    )
```
